256 devices in a mesh: seq: 32 (over z, x), tp: 8 (over y, core).
Axes of the slice: x: 4, y: 4, z: 8, core: 2. Of those that a mesh axis runs over, the one named last changes fastest.
Arguments:
- queries: bfloat16 [2048, 2048], P('seq', 'tp'), may hold values from -4.5 to 4.5
- keys: bfloat16 [16384, 2048], P('seq', 'tp'), may hold values from -4.5 to 4.5
- values: bfloat16 [16384, 2048], P('seq', 'tp'), may hold values from -24 to 24
- visible: int32 [2048], replicated, may hold values from 12290 to 16384, as said below
- out_weight: bfloat16 [2048, 2048], P('tp'), may hold values from -0.125 to 0.125
- out_cotangent: bfloat16 [2048, 2048], P('seq', 'tp'), may hold values from -24 to 24
Outputs:
- projected: bfloat16 [2048, 2048], P('seq', 'tp')
- grad_queries: float32 [2048, 2048], P('seq', 'tp')
- grad_keys: float32 [16384, 2048], P('seq', 'tp')
- grad_values: float32 [16384, 2048], P('seq', 'tp')
The draws below stay inside these ranges and needn't reach their ends.
Inputs may be any that keep to these rules, and one draw needn't show every extreme that they name: visible rises strictly with the latent index, by 1 or 2 from one latent to the next, and the last latent sees all 16384 tokens.
All inputs are finite; a program needn't handle non-finite values.
Results may differ from the reference program's by a relative error of at most 0.02.
Values may be sent and summed in bfloat16 or wider, within the bound.
A program may use at most 128 MiB of HBM per device.

```python
import math
import jax
import jax.numpy as jnp
from jax import lax

D = 2048
HEADS = 16
LATENTS = 2048
CONTEXT = 16384


def draw_keys(key, part):
    key = jax.random.fold_in(key, 11)
    drawn = jnp.clip(jax.random.normal(key, (CONTEXT, D), jnp.float32), -4.5, 4.5)
    return drawn.astype(jnp.bfloat16)


def draw_queries(key, part):
    key = jax.random.fold_in(key, 23)
    drawn = jnp.clip(3.0 * jax.random.normal(key, (LATENTS, D), jnp.float32), -4.5, 4.5)
    return drawn.astype(jnp.bfloat16)


def draw_visible(key, part):
    key = jax.random.fold_in(key, 37)
    steps_between = jax.random.randint(key, (LATENTS,), 1, 3, dtype=jnp.int32)
    after_count = jnp.cumsum(steps_between[::-1])[::-1] - steps_between
    return (CONTEXT - after_count).astype(jnp.int32)


def block_levels(rng, shape, split, smallest, high):
    loudness, own = 1.0, jax.random.fold_in(rng, 6)
    for position, blocks in split:
        steps = jnp.exp(jax.random.uniform(jax.random.fold_in(own, position), (blocks,), jnp.float32, smallest / len(split), high / len(split)))
        loudness = loudness * jnp.repeat(steps, shape[position] // blocks).reshape([-1 if axis == position else 1 for axis in range(len(shape))])
    return loudness


def centred(stream_key, extent, deviation, reach, split=(), held_as=jnp.bfloat16):
    result = jax.random.normal(stream_key, extent, jnp.float32) * deviation
    if len(split) > 0:
        result = block_levels(stream_key, extent, split, -0.22, 0.18) * result
    return jnp.clip(result, min=-reach, max=reach).astype(held_as)


def setup_inputs(seed: int = 0) -> dict:
    key_list = jax.random.split(jax.random.key(seed), 7)
    queries = draw_queries(jax.random.fold_in(key_list[6], 71), 0)
    keys = draw_keys(jax.random.fold_in(key_list[6], 71), 0)
    values = centred(key_list[2], (CONTEXT, D), 4.0, 24.0, ((0, 32), (1, 8)))
    visible = draw_visible(jax.random.fold_in(key_list[6], 71), 0)
    out_weight = centred(key_list[4], (D, D), D ** -0.5, 0.125, ((0, 8),))
    out_cotangent = centred(key_list[5], (LATENTS, D), 4.0, 24.0, ((0, 32), (1, 8)))
    return {"queries": queries, "keys": keys, "values": values, "visible": visible, "out_weight": out_weight, "out_cotangent": out_cotangent}


def reference(queries, keys, values, visible, out_weight, out_cotangent):
    head_dim = D // HEADS
    score_scale = 1.0 / math.sqrt(head_dim)
    visible_mask = jnp.arange(CONTEXT, dtype=jnp.int32)[None, :] < visible.astype(jnp.int32)[:, None]

    def split_heads(matrix, count):
        return matrix.reshape(count, HEADS, head_dim).transpose(1, 0, 2)

    def merge_heads(stacked, count):
        return stacked.transpose(1, 0, 2).reshape(count, D)

    def head_scores(query_head, key_head):
        return jnp.dot(query_head, key_head.T, preferred_element_type=jnp.float32) * score_scale

    def forward(operands):
        query_head, key_head, value_head = operands
        scores = head_scores(query_head, key_head)
        maxima = lax.optimization_barrier(jnp.max(jnp.where(visible_mask, scores, -1e+30), axis=1))
        weights = jnp.exp(jnp.where(visible_mask, scores - maxima[:, None], -jnp.inf))
        totals = lax.optimization_barrier(jnp.sum(weights, axis=1))
        numerator = jnp.dot(weights.astype(jnp.bfloat16), value_head, preferred_element_type=jnp.float32)
        return (numerator / totals[:, None], totals, maxima)
    query_heads = split_heads(queries, LATENTS)
    key_heads = split_heads(keys, CONTEXT)
    value_heads = split_heads(values, CONTEXT)
    attended_wide, totals, maxima = lax.map(forward, (query_heads, key_heads, value_heads))
    attended = merge_heads(attended_wide, LATENTS).astype(jnp.bfloat16)
    projected = jnp.dot(attended, out_weight, preferred_element_type=jnp.float32).astype(jnp.bfloat16)
    grad_attended = jnp.dot(out_cotangent, out_weight.T, preferred_element_type=jnp.float32)
    scaled_grad = (split_heads(grad_attended, LATENTS) / totals[:, :, None]).astype(jnp.bfloat16)
    attended_heads = split_heads(attended, LATENTS)

    def backward(operands):
        query_head, key_head, value_head, grad_head, output_head, maxima_head = operands
        scores = head_scores(query_head, key_head)
        weights = jnp.exp(jnp.where(visible_mask, scores - maxima_head[:, None], -jnp.inf))
        delta = lax.optimization_barrier(jnp.sum(grad_head.astype(jnp.float32) * output_head.astype(jnp.float32), axis=1))
        grad_value = jnp.dot(weights.astype(jnp.bfloat16).T, grad_head, preferred_element_type=jnp.float32)
        grad_prob = jnp.dot(grad_head, value_head.T, preferred_element_type=jnp.float32)
        grad_score = (weights * (grad_prob - delta[:, None])).astype(jnp.bfloat16)
        grad_query = jnp.dot(grad_score, key_head, preferred_element_type=jnp.float32) * score_scale
        grad_key = jnp.dot(grad_score.T, query_head, preferred_element_type=jnp.float32) * score_scale
        return (grad_query, grad_key, grad_value)
    grad_q, grad_k, grad_v = lax.map(backward, (query_heads, key_heads, value_heads, scaled_grad, attended_heads, maxima))
    return (projected, merge_heads(grad_q, LATENTS), merge_heads(grad_k, CONTEXT), merge_heads(grad_v, CONTEXT))
```

```python
import math

import jax
import jax.numpy as jnp
from jax import lax
from jax.experimental import pallas as pl
from jax.experimental.pallas import tpu as pltpu
from jax.sharding import PartitionSpec as P

HEAD = 128
NZ = 8
NX = 4
NT = 8
MESH = pl.DeviceIdType.MESH
F32 = jnp.float32
BF16 = jnp.bfloat16
NEG = -1e30
FLOOR = -1e29
SCALE = 1.0 / math.sqrt(HEAD)
EXP2_SCALE = SCALE / math.log(2.0)
LAST_LAST = (((1,), (1,)), ((), ()))


def dot(a, b):
    return jnp.dot(a, b, preferred_element_type=F32)


def dot_t(a, b):
    return lax.dot_general(a, b, LAST_LAST, preferred_element_type=F32)


def kernel(
    q_ref, k_ref, v_ref, vis_ref, wout_ref, cot_ref,
    proj_ref, gq_ref, gk_ref, gv_ref,
    qa, ga, ct, kt, vt, w, dp, sb, sz, sx, fin,
    nb, db, nx, dx, ns, ds, nz, dz, pt, pr,
    ct_s, ct_r, qz_s, qz_r, qx_s, qx_r, gz_s, gz_r, gx_s, gx_r,
    sz_s, sz_r, sx_s, sx_r, fz_s, fz_r,
    nx_s, nx_r, dx_s, dx_r, nz_s, nz_r, dz_s, dz_r, pt_s, pt_r,
):
    seq = lax.axis_index("seq")
    tp = lax.axis_index("tp")
    z0 = seq // NX
    x0 = lax.rem(seq, NX)
    rows = q_ref.shape[0]
    ctx = k_ref.shape[0]
    block = NX * rows
    heads = q_ref.shape[1] // HEAD

    def z_at(i):
        return lax.rem(z0 + i, NZ)

    def z_from(i):
        return lax.rem(z0 + NZ - i, NZ)

    def x_at(i):
        return lax.rem(x0 + i, NX)

    def t_at(i):
        return lax.rem(tp + i, NT)

    def z_dev(i):
        return {"seq": z_at(i) * NX + x0}

    def x_dev(i):
        return {"seq": z0 * NX + x_at(i)}

    def t_dev(i):
        return {"tp": t_at(i)}

    def remote(src, dst, send, recv, device):
        return pltpu.make_async_remote_copy(
            src_ref=src, dst_ref=dst, send_sem=send, recv_sem=recv,
            device_id=device, device_id_type=MESH,
        )

    def cols(h):
        return pl.ds(h * HEAD, HEAD)

    barrier = pltpu.get_barrier_semaphore()
    for count, device in ((NZ, z_dev), (NX, x_dev), (NT, t_dev)):
        @pl.loop(1, count)
        def _(i, device=device):
            pl.semaphore_signal(barrier, inc=1, device_id=device(i), device_id_type=MESH)

    for h in range(heads):
        qa[z0, x0, h] = q_ref[:, cols(h)]
    ct[tp] = cot_ref[...]
    pl.semaphore_wait(barrier, NZ + NX + NT - 3)

    def ct_copy(i):
        return remote(ct.at[tp], ct.at[tp], ct_s.at[i], ct_r.at[i], t_dev(i))

    def z_copy(buf, send, recv, i):
        return remote(buf.at[z0, x0], buf.at[z0, x0], send.at[i], recv.at[i], z_dev(i))

    def x_copy(buf, send, recv, b, i):
        return remote(buf.at[b, x0], buf.at[b, x0], send.at[b, i], recv.at[b, i], x_dev(i))

    @pl.loop(1, NT)
    def _(i):
        ct_copy(i).start()

    @pl.loop(1, NZ)
    def _(i):
        z_copy(qa, qz_s, qz_r, i).start()

    @pl.loop(1, NX)
    def _(i):
        x_copy(qa, qx_s, qx_r, z0, i).start()

    for h in range(heads):
        kt[h] = k_ref[:, cols(h)].astype(F32).T.astype(BF16)
        vt[h] = v_ref[:, cols(h)].astype(F32).T.astype(BF16)
    gk_ref[...] = jnp.zeros_like(gk_ref)
    gv_ref[...] = jnp.zeros_like(gv_ref)

    @pl.loop(1, NT)
    def _(i):
        ct_copy(i).wait_recv()

    width = cot_ref.shape[1]
    for h in range(heads):
        total = jnp.zeros((rows, HEAD), F32)
        for t in range(NT):
            total += dot_t(ct[t], wout_ref[pl.ds(h * HEAD, HEAD), t * width : (t + 1) * width])
        ga[z0, x0, h] = total.astype(BF16)

    @pl.loop(1, NZ)
    def _(i):
        z_copy(ga, gz_s, gz_r, i).start()

    @pl.loop(1, NX)
    def _(i):
        x_copy(ga, gx_s, gx_r, z0, i).start()

    @pl.loop(1, NZ)
    def _(i):
        z_copy(qa, qz_s, qz_r, i).wait_recv()

        @pl.loop(1, NX)
        def _(j):
            x_copy(qa, qx_s, qx_r, z_from(i), j).start()

    @pl.loop(1, NZ)
    def _(i):
        z_copy(ga, gz_s, gz_r, i).wait_recv()

        @pl.loop(1, NX)
        def _(j):
            x_copy(ga, gx_s, gx_r, z_from(i), j).start()

    def stat_copy(i):
        return remote(sb.at[z_at(i)], sz.at[z0], sz_s.at[i], sz_r.at[i], z_dev(i))

    position = seq * ctx + lax.broadcasted_iota(jnp.int32, (ctx, 1), 0)

    @pl.loop(0, NZ)
    def _(i):
        b = z_from(i)

        @pl.loop(1, NX)
        def _(j):
            x_copy(qa, qx_s, qx_r, b, j).wait_recv()
            x_copy(ga, gx_s, gx_r, b, j).wait_recv()

        seen = position < vis_ref[b]
        stats = []
        for h in range(heads):
            query = qa[b, :, h].reshape(block, HEAD)
            grad = ga[b, :, h].reshape(block, HEAD)
            score = jnp.where(seen, dot_t(k_ref[:, cols(h)], query), NEG)
            top = jnp.maximum(jnp.max(score, axis=0, keepdims=True), FLOOR)
            weight = jnp.exp2((score - top) * EXP2_SCALE)
            prob = dot_t(v_ref[:, cols(h)], grad)
            w[h, b] = weight
            dp[h, b] = prob
            stats += [
                top,
                jnp.sum(weight, axis=0, keepdims=True),
                jnp.sum(weight * prob, axis=0, keepdims=True),
            ]
        stats.append(jnp.zeros((8 - len(stats), block), F32))
        sb[b] = jnp.concatenate(stats, axis=0)

        @pl.when(i > 0)
        def _():
            stat_copy(NZ - i).start()

    sz[z0] = sb[z0]

    @pl.loop(1, NZ)
    def _(i):
        stat_copy(i).wait_recv()

    def merged(ref):
        out = []
        for h in range(heads):
            tops = ref[:, 3 * h]
            top = jnp.max(tops, axis=0, keepdims=True)
            factor = jnp.exp2((tops - top) * EXP2_SCALE)
            out += [
                top,
                jnp.sum(ref[:, 3 * h + 1] * factor, axis=0, keepdims=True),
                jnp.sum(ref[:, 3 * h + 2] * factor, axis=0, keepdims=True),
            ]
        return out

    pad = jnp.zeros((8 - 3 * heads, block), F32)
    sx[x0] = jnp.concatenate(merged(sz) + [pad], axis=0)

    def stat_x_copy(i):
        return remote(sx.at[x0], sx.at[x0], sx_s.at[i], sx_r.at[i], x_dev(i))

    @pl.loop(1, NX)
    def _(i):
        stat_x_copy(i).start()

    @pl.loop(1, NX)
    def _(i):
        stat_x_copy(i).wait_recv()

    whole = merged(sx)
    final = []
    for h in range(heads):
        top, total, product = whole[3 * h : 3 * h + 3]
        final += [top * EXP2_SCALE + jnp.log2(total), product / total]
    final.append(jnp.zeros((8 - len(final), block), F32))
    fin[z0] = jnp.concatenate(final, axis=0)

    def fin_copy(i):
        return remote(fin.at[z0], fin.at[z0], fz_s.at[i], fz_r.at[i], z_dev(i))

    @pl.loop(1, NZ)
    def _(i):
        fin_copy(i).start()

    def nx_copy(b, i):
        return remote(nb.at[b, x_at(i)], nx.at[b, x0], nx_s.at[b, i], nx_r.at[b, i], x_dev(i))

    def dx_copy(b, i):
        return remote(db.at[b, x_at(i)], dx.at[b, x0], dx_s.at[b, i], dx_r.at[b, i], x_dev(i))

    @pl.loop(0, NZ)
    def _(i):
        b = z_from(i)

        @pl.when(i > 0)
        def _():
            fin_copy(i).wait_recv()

        for h in range(heads):
            log_total = fin[b, 2 * h : 2 * h + 1]
            factor = jnp.exp2(sb[b, 3 * h : 3 * h + 1] * EXP2_SCALE - log_total)
            weight = w[h, b] * factor
            w[h, b] = weight
            low = weight.astype(BF16)
            term = dot(vt[h], low).T.astype(BF16)
            nb[b, :, h] = term.reshape(NX, rows, HEAD)
            gv_ref[:, cols(h)] += dot(low, ga[b, :, h].reshape(block, HEAD))

        @pl.loop(1, NX)
        def _(j):
            nx_copy(b, j).start()

    @pl.loop(0, NZ)
    def _(i):
        b = z_from(i)
        for h in range(heads):
            delta = fin[b, 2 * h + 1 : 2 * h + 2]
            low = (w[h, b] * (dp[h, b] - delta)).astype(BF16)
            term = (dot(kt[h], low) * SCALE).T.astype(BF16)
            db[b, :, h] = term.reshape(NX, rows, HEAD)
            gk_ref[:, cols(h)] += dot(low, qa[b, :, h].reshape(block, HEAD))

        @pl.loop(1, NX)
        def _(j):
            dx_copy(b, j).start()

    gk_ref[...] = gk_ref[...] * SCALE

    def nz_copy(i):
        return remote(ns.at[z_at(i)], nz.at[z0], nz_s.at[i], nz_r.at[i], z_dev(i))

    def dz_copy(i):
        return remote(ds.at[z_at(i)], dz.at[z0], dz_s.at[i], dz_r.at[i], z_dev(i))

    def reduce_x(own, got, out, x_copies, z_copies):
        @pl.loop(0, NZ)
        def _(i):
            b = z_from(i)

            @pl.loop(1, NX)
            def _(j):
                x_copies(b, j).wait_recv()

            total = own[b, x0].astype(F32)
            for j in range(1, NX):
                total += got[b, x_at(j)].astype(F32)
            out[b] = total.astype(BF16)

            @pl.when(i > 0)
            def _():
                z_copies(NZ - i).start()

    def reduce_z(own, got, z_copies):
        @pl.loop(1, NZ)
        def _(i):
            z_copies(i).wait_recv()

        got[z0] = own[z0]
        total = got[0].astype(F32)
        for j in range(1, NZ):
            total += got[j].astype(F32)
        return total

    reduce_x(nb, nx, ns, nx_copy, nz_copy)
    attended = reduce_z(ns, nz, nz_copy).astype(BF16)

    def pt_copy(i):
        return remote(pt.at[t_at(i)], pr.at[tp], pt_s.at[i], pt_r.at[i], t_dev(i))

    for t in range(NT):
        term = jnp.zeros((rows, width), F32)
        for h in range(heads):
            term += dot(attended[h], wout_ref[pl.ds(h * HEAD, HEAD), t * width : (t + 1) * width])
        pt[t] = term.astype(BF16)

    @pl.loop(1, NT)
    def _(i):
        pt_copy(i).start()

    reduce_x(db, dx, ds, dx_copy, dz_copy)

    @pl.loop(1, NT)
    def _(i):
        pt_copy(i).wait_recv()

    pr[tp] = pt[tp]
    total = pr[0].astype(F32)
    for t in range(1, NT):
        total += pr[t].astype(F32)
    proj_ref[...] = total.astype(BF16)

    grad = reduce_z(ds, dz, dz_copy)
    for h in range(heads):
        gq_ref[:, cols(h)] = grad[h]

    @pl.loop(1, NT)
    def _(i):
        ct_copy(i).wait_send()
        pt_copy(i).wait_send()

    @pl.loop(1, NZ)
    def _(i):
        z_copy(qa, qz_s, qz_r, i).wait_send()
        z_copy(ga, gz_s, gz_r, i).wait_send()
        stat_copy(i).wait_send()
        fin_copy(i).wait_send()
        nz_copy(i).wait_send()
        dz_copy(i).wait_send()

    @pl.loop(1, NX)
    def _(j):
        stat_x_copy(j).wait_send()

        @pl.loop(0, NZ)
        def _(b):
            x_copy(qa, qx_s, qx_r, b, j).wait_send()
            x_copy(ga, gx_s, gx_r, b, j).wait_send()
            nx_copy(b, j).wait_send()
            dx_copy(b, j).wait_send()


def body(queries, keys, values, visible, out_weight, out_cotangent):
    rows, width = queries.shape
    ctx = keys.shape[0]
    heads = width // HEAD
    block = NX * rows
    vmem = pl.BlockSpec(memory_space=pltpu.VMEM)
    sem = pltpu.SemaphoreType.DMA
    return pl.pallas_call(
        kernel,
        out_shape=(
            jax.ShapeDtypeStruct((rows, width), BF16),
            jax.ShapeDtypeStruct((rows, width), F32),
            jax.ShapeDtypeStruct((ctx, width), F32),
            jax.ShapeDtypeStruct((ctx, width), F32),
        ),
        in_specs=[vmem] * 6,
        out_specs=[vmem] * 4,
        scratch_shapes=[
            pltpu.VMEM((NZ, NX, heads, rows, HEAD), BF16),
            pltpu.VMEM((NZ, NX, heads, rows, HEAD), BF16),
            pltpu.VMEM((NT, rows, width), BF16),
            pltpu.VMEM((heads, HEAD, ctx), BF16),
            pltpu.VMEM((heads, HEAD, ctx), BF16),
            pltpu.VMEM((heads, NZ, ctx, block), F32),
            pltpu.VMEM((heads, NZ, ctx, block), F32),
            pltpu.VMEM((NZ, 8, block), F32),
            pltpu.VMEM((NZ, 8, block), F32),
            pltpu.VMEM((NX, 8, block), F32),
            pltpu.VMEM((NZ, 8, block), F32),
            pltpu.VMEM((NZ, NX, heads, rows, HEAD), BF16),
            pltpu.VMEM((NZ, NX, heads, rows, HEAD), BF16),
            pltpu.VMEM((NZ, NX, heads, rows, HEAD), BF16),
            pltpu.VMEM((NZ, NX, heads, rows, HEAD), BF16),
            pltpu.VMEM((NZ, heads, rows, HEAD), BF16),
            pltpu.VMEM((NZ, heads, rows, HEAD), BF16),
            pltpu.VMEM((NZ, heads, rows, HEAD), BF16),
            pltpu.VMEM((NZ, heads, rows, HEAD), BF16),
            pltpu.VMEM((NT, rows, width), BF16),
            pltpu.VMEM((NT, rows, width), BF16),
            sem((NT,)), sem((NT,)),
            sem((NZ,)), sem((NZ,)), sem((NZ, NX)), sem((NZ, NX)),
            sem((NZ,)), sem((NZ,)), sem((NZ, NX)), sem((NZ, NX)),
            sem((NZ,)), sem((NZ,)), sem((NX,)), sem((NX,)), sem((NZ,)), sem((NZ,)),
            sem((NZ, NX)), sem((NZ, NX)), sem((NZ, NX)), sem((NZ, NX)),
            sem((NZ,)), sem((NZ,)), sem((NZ,)), sem((NZ,)),
            sem((NT,)), sem((NT,)),
        ],
        compiler_params=pltpu.CompilerParams(
            collective_id=0, has_side_effects=True, vmem_limit_bytes=56 * 2**20
        ),
    )(queries, keys, values, visible.reshape(NZ, 1, block), out_weight, out_cotangent)


def solution(mesh):
    return jax.shard_map(
        body,
        mesh=mesh,
        in_specs=(
            P("seq", "tp"),
            P("seq", "tp"),
            P("seq", "tp"),
            P(),
            P("tp", None),
            P("seq", "tp"),
        ),
        out_specs=(P("seq", "tp"), P("seq", "tp"), P("seq", "tp"), P("seq", "tp")),
        check_vma=False,
    )
```

```python
import math

import jax
import jax.numpy as jnp
from jax import lax
from jax.experimental import pallas as pl
from jax.experimental.pallas import tpu as pltpu
from jax.sharding import PartitionSpec as P

HEAD = 128
NZ = 8
NX = 4
NT = 8
MESH = pl.DeviceIdType.MESH
F32 = jnp.float32
BF16 = jnp.bfloat16
NEG = -1e30
FLOOR = -1024.0
LEVEL_ROWS = 16
NEAR = (1, 7, 2, 6, 3, 5, 4)
CHAINS = ((0, 1, 4), (0, -1, 3), (1, 1, 3), (1, -1, 4))
SCALE = 1.0 / math.sqrt(HEAD)
EXP2_SCALE = SCALE / math.log(2.0)
LAST_LAST = (((1,), (1,)), ((), ()))


def dot(a, b):
    return jnp.dot(a, b, preferred_element_type=F32)


def dot_t(a, b):
    return lax.dot_general(a, b, LAST_LAST, preferred_element_type=F32)


def kernel(
    q_hbm, k_hbm, v_hbm, vis_hbm, wout_hbm, cot_hbm,
    proj_ref, gq_ref, gk_ref, gv_ref,
    k_ref, v_ref, vis_ref, wout_ref, in_s,
    qa, ga, ct, kt, vt, w, dp, nu, sb, sz, sx, fin,
    ring_out, ring_in, nb, nx, db, dx, ds, dz, pt, pr,
    ct_s, ct_r, qx_s, qx_r, qz_s, qz_r, gz_s, gz_r, gx_s, gx_r,
    sz_s, sz_r, sx_s, sx_r, fz_s, fz_r,
    rn_s, rn_r, nx_s, nx_r, dx_s, dx_r, dz_s, dz_r, pt_s, pt_r,
):
    seq = lax.axis_index("seq")
    tp = lax.axis_index("tp")
    z0 = seq // NX
    x0 = lax.rem(seq, NX)
    rows, width = q_hbm.shape
    ctx = k_hbm.shape[0]
    block = NX * rows
    heads = width // HEAD

    def z_at(i):
        return lax.rem(z0 + i, NZ)

    def z_from(i):
        return lax.rem(z0 + NZ - i, NZ)

    def x_at(i):
        return lax.rem(x0 + i, NX)

    def t_at(i):
        return lax.rem(tp + i, NT)

    def z_dev(i):
        return {"seq": z_at(i) * NX + x0}

    def x_dev(i):
        return {"seq": z0 * NX + x_at(i)}

    def t_dev(i):
        return {"tp": t_at(i)}

    def remote(src, dst, send, recv, device):
        return pltpu.make_async_remote_copy(
            src_ref=src, dst_ref=dst, send_sem=send, recv_sem=recv,
            device_id=device, device_id_type=MESH,
        )

    def cols(h):
        return pl.ds(h * HEAD, HEAD)

    def take(ref, sem):
        remote(ref, ref, sem, sem, {"tp": tp}).wait_recv()

    def sent(ref, sem):
        remote(ref, ref, sem, sem, {"tp": tp}).wait_send()

    def but_one(ref):
        return ref.at[pl.ds(0, ref.shape[0] - 1)]

    def each(count, action):
        @pl.loop(1, count)
        def _(i):
            action(i)

    loads = [
        pltpu.make_async_copy(src, dst, in_s.at[i])
        for i, (src, dst) in enumerate(
            [(q_hbm.at[:, cols(h)], qa.at[z0, h, x0]) for h in range(heads)]
            + [(cot_hbm, ct.at[tp]), (k_hbm, k_ref), (v_hbm, v_ref), (wout_hbm, wout_ref), (vis_hbm, vis_ref)]
        )
    ]
    for load in loads:
        load.start()

    barrier = pltpu.get_barrier_semaphore()
    for count, device in ((NZ, z_dev), (NX, x_dev), (NT, t_dev)):
        @pl.loop(1, count)
        def _(i, device=device):
            pl.semaphore_signal(barrier, inc=1, device_id=device(i), device_id_type=MESH)

    for load in loads[: heads + 1]:
        load.wait()
    pl.semaphore_wait(barrier, NZ + NX + NT - 3)

    def ct_copy(i):
        return remote(ct.at[tp], ct.at[tp], ct_s, ct_r, t_dev(i))

    def qx_copy(i):
        return remote(qa.at[z0, :, x0], qa.at[z0, :, x0], qx_s, qx_r, x_dev(i))

    def qz_copy(chain, n):
        h, sign, _ = CHAINS[chain]
        part = qa.at[z_from(sign * (n - 1)), h]
        return remote(part, part, qz_s.at[h], qz_r.at[chain, n - 1], z_dev(NZ + sign))

    def gz_copy(i):
        return remote(ga.at[z0, :, x0], ga.at[z0, :, x0], gz_s, gz_r.at[i], z_dev(i))

    def gx_copy(b, i):
        return remote(ga.at[b, :, x0], ga.at[b, :, x0], gx_s, gx_r.at[b], x_dev(i))

    each(NT, lambda i: ct_copy(i).start())
    each(NX, lambda i: qx_copy(i).start())

    for load in loads[heads + 1 :]:
        load.wait()
    for h in range(heads):
        kt[h] = k_ref[:, cols(h)].astype(F32).T.astype(BF16)
        vt[h] = v_ref[:, cols(h)].astype(F32).T.astype(BF16)

    take(qa.at[0, :, pl.ds(0, NX - 1)], qx_r)
    for chain in range(len(CHAINS)):
        qz_copy(chain, 1).start()

    sb[...] = jnp.zeros_like(sb)
    gk_ref[...] = jnp.zeros_like(gk_ref)
    gv_ref[...] = jnp.zeros_like(gv_ref)

    take(but_one(ct), ct_r)
    for h in range(heads):
        total = jnp.zeros((rows, HEAD), F32)
        for t in range(NT):
            total += dot_t(ct[t], wout_ref[pl.ds(h * HEAD, HEAD), t * width : (t + 1) * width])
        ga[z0, h, x0] = total.astype(BF16)
    each(NX, lambda i: gx_copy(z0, i).start())
    for i in NEAR:
        gz_copy(i).start()

    position = seq * ctx + lax.broadcasted_iota(jnp.int32, (ctx, 1), 0)

    def weigh(b):
        seen = position < vis_ref[b]
        for h in range(heads):
            score = jnp.where(seen, dot_t(k_ref[:, cols(h)], qa[b, h].reshape(block, HEAD)), NEG)
            top = jnp.max(score, axis=0, keepdims=True) * EXP2_SCALE
            level = jnp.ceil(jnp.maximum(top, FLOOR) * 0.25) * 4.0
            weight = jnp.exp2(score * EXP2_SCALE - level)
            w[h, b] = weight
            nu[h, b] = dot(vt[h], weight.astype(BF16))
            sb[b, pl.ds(3 * h, 1)] = level
            sb[b, pl.ds(3 * h + 1, 1)] = jnp.sum(weight, axis=0, keepdims=True)

    def pass_on(i):
        gz_copy(i).wait_recv()
        each(NX, lambda j: gx_copy(z_from(i), j).start())

    @pl.loop(1, NZ // 2 + 1)
    def _(n):
        for chain, (_, _, hops) in enumerate(CHAINS):
            @pl.when(n <= hops)
            def _(chain=chain):
                qz_copy(chain, n).wait_recv()

            @pl.when(n < hops)
            def _(chain=chain):
                qz_copy(chain, n + 1).start()

        @pl.when(n == 1)
        def _():
            for i in NEAR[:4]:
                pass_on(i)

        @pl.when(n == 2)
        def _():
            for i in NEAR[4:]:
                pass_on(i)

        weigh(z_from(n - 1))

        @pl.when(n > 1)
        def _():
            weigh(z_at(n - 1))

    weigh(z_at(NZ // 2))

    def ring_slot(chain, n):
        return n - 1 + CHAINS[chain - 1][2] * (chain % 2)

    def ring_copy(chain, n):
        h, sign, _ = CHAINS[chain]
        slot = ring_slot(chain, n)
        return remote(
            ring_out.at[h, slot], ring_in.at[h, slot],
            rn_s.at[h], rn_r.at[h, slot], z_dev(NZ + sign),
        )

    def arrived(chain, n):
        ring_copy(chain, n).wait_recv()
        h, slot = CHAINS[chain][0], ring_slot(chain, n)
        return (
            ring_in[h, slot, pl.ds(0, HEAD)].astype(F32),
            ring_in[h, slot, pl.ds(HEAD, LEVEL_ROWS)].astype(F32)[:1],
        )

    def own_part(h, b):
        return nu[h, b], sb[b, pl.ds(3 * h, 1)]

    def joined(parts):
        level = parts[0][1]
        for _, other in parts[1:]:
            level = jnp.maximum(level, other)
        total = sum(part * jnp.exp2(other - level) for part, other in parts)
        return total, level

    def ring_step(chain, n):
        h, sign, hops = CHAINS[chain]
        parts = [own_part(h, z_at(NZ + sign * n))]
        if n < hops:
            parts.append(arrived(chain, n + 1))
        total, level = joined(parts)
        slot = ring_slot(chain, n)
        ring_out[h, slot, pl.ds(0, HEAD)] = total.astype(BF16)
        ring_out[h, slot, pl.ds(HEAD, LEVEL_ROWS)] = jnp.broadcast_to(level, (LEVEL_ROWS, block)).astype(BF16)
        ring_copy(chain, n).start()

    for chain, (_, _, hops) in enumerate(CHAINS):
        ring_step(chain, hops)

    def stat_copy(i):
        return remote(sb.at[z_at(i)], sz.at[z0], sz_s, sz_r, z_dev(i))

    @pl.loop(0, NZ)
    def _(i):
        odd = lax.rem(i, 2)
        off = odd * ((i + 1) // 2) + (1 - odd) * lax.rem(NZ - i // 2, NZ)
        b = z_from(off)
        take(ga.at[b, :, pl.ds(0, NX - 1)], gx_r.at[b])
        for h in range(heads):
            prob = dot_t(v_ref[:, cols(h)], ga[b, h].reshape(block, HEAD))
            dp[h, b] = prob
            sb[b, pl.ds(3 * h + 2, 1)] = jnp.sum(w[h, b] * prob, axis=0, keepdims=True)

        @pl.when(i > 0)
        def _():
            stat_copy(NZ - off).start()

    for chain, (_, _, hops) in enumerate(CHAINS):
        if hops == NZ // 2:
            ring_step(chain, hops - 1)

    sz[z0] = sb[z0]
    take(but_one(sz), sz_r)

    def merged(ref):
        out = []
        for h in range(heads):
            tops = ref[:, 3 * h]
            top = jnp.max(tops, axis=0, keepdims=True)
            factor = jnp.exp2(tops - top)
            out += [
                top,
                jnp.sum(ref[:, 3 * h + 1] * factor, axis=0, keepdims=True),
                jnp.sum(ref[:, 3 * h + 2] * factor, axis=0, keepdims=True),
            ]
        return out

    pad = jnp.zeros((8 - 3 * heads, block), F32)
    sx[x0] = jnp.concatenate(merged(sz) + [pad], axis=0)

    def stat_x_copy(i):
        return remote(sx.at[x0], sx.at[x0], sx_s, sx_r, x_dev(i))

    each(NX, lambda i: stat_x_copy(i).start())
    for chain in range(len(CHAINS)):
        ring_step(chain, 2)
    take(but_one(sx), sx_r)

    whole = merged(sx)
    final = []
    for h in range(heads):
        top, total, product = whole[3 * h : 3 * h + 3]
        final += [top + jnp.log2(total), product / total]
    final.append(jnp.zeros((8 - len(final), block), F32))
    fin[z0] = jnp.concatenate(final, axis=0)

    def fin_copy(i):
        return remote(fin.at[z0], fin.at[z0], fz_s, fz_r, z_dev(i))

    each(NZ, lambda i: fin_copy(i).start())
    for chain in range(len(CHAINS)):
        ring_step(chain, 1)

    def nx_copy(i):
        return remote(nb.at[x_at(i)], nx.at[x0], nx_s, nx_r, x_dev(i))

    def dx_copy(b, i):
        return remote(db.at[b, x_at(i)], dx.at[b, x0], dx_s, dx_r.at[b], x_dev(i))

    def backward(first, last):
        @pl.loop(first, last)
        def _(i):
            b = z_from(i)

            for h in range(heads):
                factor = jnp.exp2(sb[b, pl.ds(3 * h, 1)] - fin[b, pl.ds(2 * h, 1)])
                weight = w[h, b] * factor
                low = weight.astype(BF16)
                grad = (weight * (dp[h, b] - fin[b, pl.ds(2 * h + 1, 1)])).astype(BF16)
                term = (dot(kt[h], grad) * SCALE).T.astype(BF16)
                db[b, :, h] = term.reshape(NX, rows, HEAD)
                gk_ref[:, cols(h)] += dot(grad, qa[b, h].reshape(block, HEAD))
                gv_ref[:, cols(h)] += dot(low, ga[b, h].reshape(block, HEAD))
            each(NX, lambda j: dx_copy(b, j).start())

    take(but_one(fin), fz_r)
    backward(0, NZ // 2)
    for h in range(heads):
        parts = [own_part(h, z0)]
        for chain, (head, _, _) in enumerate(CHAINS):
            if head == h:
                parts.append(arrived(chain, 1))
        total, level = joined(parts)
        total = total * jnp.exp2(level - fin[z0, pl.ds(2 * h, 1)])
        nb[:, h] = total.T.astype(BF16).reshape(NX, rows, HEAD)
    each(NX, lambda i: nx_copy(i).start())
    backward(NZ // 2, NZ)
    gk_ref[...] = gk_ref[...] * SCALE

    take(but_one(nx), nx_r)
    total = nb[x0].astype(F32)
    for j in range(1, NX):
        total += nx[x_at(j)].astype(F32)
    attended = total.astype(BF16)

    def pt_copy(i):
        return remote(pt.at[t_at(i)], pr.at[tp], pt_s, pt_r, t_dev(i))

    for t in range(NT):
        term = jnp.zeros((rows, width), F32)
        for h in range(heads):
            term += dot(attended[h], wout_ref[pl.ds(h * HEAD, HEAD), t * width : (t + 1) * width])
        pt[t] = term.astype(BF16)
    each(NT, lambda i: pt_copy(i).start())

    def dz_copy(i):
        return remote(ds.at[z_at(i)], dz.at[z0], dz_s, dz_r, z_dev(i))

    @pl.loop(0, NZ)
    def _(i):
        b = z_from(i)
        take(but_one(dx.at[b]), dx_r.at[b])
        total = db[b, x0].astype(F32)
        for j in range(1, NX):
            total += dx[b, x_at(j)].astype(F32)
        ds[b] = total.astype(BF16)

        @pl.when(i > 0)
        def _():
            dz_copy(NZ - i).start()

    take(but_one(pr), pt_r)
    pr[tp] = pt[tp]
    total = pr[0].astype(F32)
    for t in range(1, NT):
        total += pr[t].astype(F32)
    proj_ref[...] = total.astype(BF16)

    take(but_one(dz), dz_r)
    dz[z0] = ds[z0]
    total = dz[0].astype(F32)
    for j in range(1, NZ):
        total += dz[j].astype(F32)
    for h in range(heads):
        gq_ref[:, cols(h)] = total[h]

    sent(but_one(ct), ct_s)
    sent(but_one(pt), pt_s)
    sent(qa.at[0, :, pl.ds(0, NX - 1)], qx_s)
    sent(ga.at[pl.ds(0, NZ - 1), :, 0], gz_s)
    sent(ga.at[:, :, pl.ds(0, NX - 1)], gx_s)
    sent(but_one(sb), sz_s)
    sent(but_one(sx), sx_s)
    sent(but_one(fin), fz_s)
    sent(but_one(nb), nx_s)
    sent(db.at[:, pl.ds(0, NX - 1)], dx_s)
    sent(but_one(ds), dz_s)
    for h in range(heads):
        sent(qa.at[pl.ds(0, NZ - 1), h], qz_s.at[h])
        sent(ring_out.at[h, pl.ds(0, NZ - 1)], rn_s.at[h])


def hand_over(*refs):
    sems = refs[8]
    copies = [pltpu.make_async_copy(refs[i], refs[4 + i], sems.at[i]) for i in range(4)]
    for copy in copies:
        copy.start()
    for copy in copies:
        copy.wait()


def body(queries, keys, values, visible, out_weight, out_cotangent):
    rows, width = queries.shape
    ctx = keys.shape[0]
    heads = width // HEAD
    block = NX * rows
    vmem = pl.BlockSpec(memory_space=pltpu.VMEM)
    hbm = pl.BlockSpec(memory_space=pl.ANY)
    sem = pltpu.SemaphoreType.DMA
    outs = pl.pallas_call(
        kernel,
        out_shape=(
            pltpu.VMEM((rows, width), BF16),
            pltpu.VMEM((rows, width), F32),
            pltpu.VMEM((ctx, width), F32),
            pltpu.VMEM((ctx, width), F32),
        ),
        in_specs=[hbm] * 6,
        out_specs=[vmem] * 4,
        scratch_shapes=[
            pltpu.VMEM((ctx, width), BF16),
            pltpu.VMEM((ctx, width), BF16),
            pltpu.VMEM((NZ, 1, block), jnp.int32),
            pltpu.VMEM(out_weight.shape, BF16),
            sem((heads + 5,)),
            pltpu.VMEM((NZ, heads, NX, rows, HEAD), BF16),
            pltpu.VMEM((NZ, heads, NX, rows, HEAD), BF16),
            pltpu.VMEM((NT, rows, width), BF16),
            pltpu.VMEM((heads, HEAD, ctx), BF16),
            pltpu.VMEM((heads, HEAD, ctx), BF16),
            pltpu.VMEM((heads, NZ, ctx, block), F32),
            pltpu.VMEM((heads, NZ, ctx, block), F32),
            pltpu.VMEM((heads, NZ, HEAD, block), F32),
            pltpu.VMEM((NZ, 8, block), F32),
            pltpu.VMEM((NZ, 8, block), F32),
            pltpu.VMEM((NX, 8, block), F32),
            pltpu.VMEM((NZ, 8, block), F32),
            pltpu.VMEM((heads, NZ - 1, HEAD + LEVEL_ROWS, block), BF16),
            pltpu.VMEM((heads, NZ - 1, HEAD + LEVEL_ROWS, block), BF16),
            pltpu.VMEM((NX, heads, rows, HEAD), BF16),
            pltpu.VMEM((NX, heads, rows, HEAD), BF16),
            pltpu.VMEM((NZ, NX, heads, rows, HEAD), BF16),
            pltpu.VMEM((NZ, NX, heads, rows, HEAD), BF16),
            pltpu.VMEM((NZ, heads, rows, HEAD), BF16),
            pltpu.VMEM((NZ, heads, rows, HEAD), BF16),
            pltpu.VMEM((NT, rows, width), BF16),
            pltpu.VMEM((NT, rows, width), BF16),
            sem, sem,
            sem, sem, sem((heads,)), sem((len(CHAINS), NZ // 2)),
            sem, sem((NZ,)), sem, sem((NZ,)),
            sem, sem, sem, sem, sem, sem,
            sem((heads,)), sem((heads, NZ - 1)),
            sem, sem, sem, sem((NZ,)),
            sem, sem,
            sem, sem,
        ],
        compiler_params=pltpu.CompilerParams(
            collective_id=0, has_side_effects=True, vmem_limit_bytes=56 * 2**20
        ),
    )(queries, keys, values, visible.reshape(NZ, 1, block), out_weight, out_cotangent)
    return pl.pallas_call(
        hand_over,
        out_shape=tuple(jax.ShapeDtypeStruct(o.shape, o.dtype) for o in outs),
        in_specs=[vmem] * 4,
        out_specs=[hbm] * 4,
        scratch_shapes=[sem((4,))],
    )(*(pltpu.with_memory_space_constraint(o, pltpu.VMEM) for o in outs))


def solution(mesh):
    return jax.shard_map(
        body,
        mesh=mesh,
        in_specs=(
            P("seq", "tp"),
            P("seq", "tp"),
            P("seq", "tp"),
            P(),
            P("tp", None),
            P("seq", "tp"),
        ),
        out_specs=(P("seq", "tp"), P("seq", "tp"), P("seq", "tp"), P("seq", "tp")),
        check_vma=False,
    )
```
